128 devices in a mesh: row: 16 (over x_hi, z, core), col: 8 (over y, x_lo).
Axes of the slice: x: 4 (x_hi: 2, x_lo: 2; x = x_hi * 2 + x_lo), y: 4, z: 4, core: 2. Of those that a mesh axis runs over, the one named last changes fastest.
Arguments:
- density: float32 [128, 16, 128, 128], P('row', 'col'), as said below
- hamiltonian: float32 [128, 16, 128, 128], P('row', 'col'), as said below
- neighbours: int32 [128, 16], P('row'), may hold values from 0 to 127, as said below
Outputs:
- new_density: float32 [128, 16, 128, 128], P('row', 'col')
- energy_density: float32 [128, 16, 128, 128], P('row', 'col')
The draws below stay inside these ranges and needn't reach their ends.
Inputs may be any that keep to these rules, and one draw needn't show every extreme that they name: `neighbours`: every entry of row I is a block column within 7 of I, cyclically over 128; each row lists its own index I, entries that name no neighbour repeat I, and row I lists J exactly when row J lists I. `density`: the matrix that these blocks form is symmetric. `hamiltonian`: the matrix that these blocks form is symmetric.
All inputs are finite; a program needn't handle non-finite values.
Results may differ from the reference program's by a relative error of at most 0.0001.
Values sent between devices are 32-bit elements; how exact they have to be, the bound alone decides.
A program may use at most 192 MiB of HBM per device.

```python
import math
import jax
import jax.numpy as jnp
from jax import lax

BS = 128
W = 8
S = 16
NB = 128
N_COL = 8


def block_grid():
    row_grid = jnp.arange(NB, dtype=jnp.int32)[:, None] * jnp.ones((1, S), jnp.int32)
    slot_grid = jnp.ones((NB, 1), jnp.int32) * jnp.arange(S, dtype=jnp.int32)[None, :]
    return (row_grid, slot_grid)


def paired_blocks(key, scale, spread):
    per_class = S // N_COL
    row_grid, slot_grid = block_grid()
    cols = (row_grid - W + (slot_grid // per_class - row_grid + W) % N_COL + slot_grid % per_class * N_COL) % NB
    lower = jnp.minimum(row_grid, cols)
    upper = jnp.maximum(row_grid, cols)
    pair_ids = (lower * NB + upper).reshape(-1)
    flipped = (row_grid > cols).reshape(-1)
    diagonal = (row_grid == cols).reshape(-1)

    def one_block(pair_id, flip, on_diagonal):
        values = jax.random.normal(jax.random.fold_in(key, pair_id), (BS, BS), jnp.float32)
        mirrored = (values + values.T) / math.sqrt(2.0)
        return jnp.where(on_diagonal, mirrored, jnp.where(flip, values.T, values))
    blocks = jax.vmap(one_block)(pair_ids, flipped, diagonal).reshape(NB, S, BS, BS)
    row_scale = jnp.exp(jax.random.uniform(jax.random.fold_in(key, 999983), (NB,), jnp.float32, -math.log(spread), 1e-09))
    pair_scale = jnp.sqrt(row_scale[row_grid] * row_scale[cols])
    return blocks * (scale * pair_scale)[:, :, None, None]


def draw_density(key, part):
    key = jax.random.fold_in(key, 11)
    spread = 1.0
    return paired_blocks(key, 0.5 * (S * BS) ** (-0.25), spread)


def draw_hamiltonian(key, part):
    key = jax.random.fold_in(key, 13)
    spread = 1.0
    return paired_blocks(key, 4.0 * (S * BS) ** (-0.5), spread)


def draw_neighbours(key, part):
    key = jax.random.fold_in(key, 5)
    row_grid, slot_grid = block_grid()
    cols = (row_grid - W + slot_grid) % NB
    lower = jnp.minimum(row_grid, cols)
    upper = jnp.maximum(row_grid, cols)
    pair_ids = (lower * NB + upper).reshape(-1)
    chances = jax.vmap(lambda pair_id: jax.random.randint(jax.random.fold_in(key, pair_id), (), 0, 8))(pair_ids)
    chances = chances.reshape(NB, S)
    threshold = 2 + lower * 6 // NB
    listed = (slot_grid == W) | (slot_grid > 0) & (chances < threshold)
    return jnp.where(listed, cols, row_grid).astype(jnp.int32)


def setup_inputs(seed: int = 0) -> dict:
    streams_of = jax.random.split(jax.random.key(seed), 4)
    density = draw_density(jax.random.fold_in(streams_of[3], 71), 0)
    hamiltonian = draw_hamiltonian(jax.random.fold_in(streams_of[3], 71), 0)
    neighbours = draw_neighbours(jax.random.fold_in(streams_of[3], 71), 0)
    return dict(density=density, hamiltonian=hamiltonian, neighbours=neighbours)


def shift_slots(blocks, amount):
    width = blocks.shape[1]
    if amount >= 0:
        kept = blocks[:, amount:]
        filler = jnp.zeros((blocks.shape[0], amount) + blocks.shape[2:], blocks.dtype)
        return jnp.concatenate([kept, filler], axis=1)
    kept = blocks[:, :width + amount]
    filler = jnp.zeros((blocks.shape[0], -amount) + blocks.shape[2:], blocks.dtype)
    return jnp.concatenate([filler, kept], axis=1)


def band_product(left_band, right_band, listed):
    result = jnp.zeros(left_band.shape, jnp.float32)
    for offset in range(S):
        moved = shift_slots(jnp.roll(right_band, W - offset, axis=0), W - offset)
        result = result + jnp.einsum("iab,iebc->ieac", left_band[:, offset], moved,
                                     precision=lax.Precision.HIGHEST)
    return result * listed[:, :, None, None]


def reference(density, hamiltonian, neighbours):
    per_class = S // N_COL
    row_grid = jnp.arange(NB, dtype=jnp.int32)[:, None]
    slot_grid = jnp.arange(S, dtype=jnp.int32)[None, :]
    to_band = ((slot_grid + row_grid - W) % N_COL) * per_class + slot_grid // N_COL
    to_class = ((slot_grid // per_class - row_grid + W) % N_COL) + (slot_grid % per_class) * N_COL
    band_cols = (row_grid - W + slot_grid) % NB
    listed = jnp.any(neighbours[:, None, :] == band_cols[:, :, None], axis=2).astype(jnp.float32)

    def banded(blocks):
        return jnp.take_along_axis(blocks, to_band[:, :, None, None].astype(jnp.int32), axis=1)

    def classed(blocks):
        return jnp.take_along_axis(blocks, to_class[:, :, None, None].astype(jnp.int32), axis=1)

    masked_density = banded(density) * listed[:, :, None, None]
    masked_hamiltonian = banded(hamiltonian) * listed[:, :, None, None]
    squared = band_product(masked_density, masked_density, listed)
    mixed = band_product(masked_hamiltonian, masked_density, listed)
    cubed = band_product(masked_density, squared, listed)
    energy_density = band_product(masked_density, mixed, listed)
    new_density = 3.0 * squared - 2.0 * cubed
    return classed(new_density), classed(energy_density)
```

```python
import functools
import jax
import jax.numpy as jnp
from jax import lax
from jax.experimental import pallas as pl
from jax.experimental.pallas import tpu as pltpu
from jax.sharding import PartitionSpec as P

MESH = pl.DeviceIdType.MESH
F32 = jnp.float32
BF16 = jnp.bfloat16
R8 = 8
N_ROW = 16
NB = 128
BW = 15
MID = 7
HALF = 4
GROUP = 3


def class_of(c, delta):
    if delta & 1:
        c = c + 1 - 2 * (c % 2)
    if delta & 2:
        c = c + 2 * (1 - 2 * ((c // 2) % 2))
    if delta & 4:
        c = c % 2 + 6 - 2 * (c // 2)
    return c


def slot_row(k, slot):
    e = slot - 4 * (slot // 5)
    wrap = (k + e) // 8
    i = (k + e) % 8
    is_off = slot // 5
    is_four = slot // 4 - is_off
    off = is_off * (1 - 2 * wrap) - is_four * wrap
    return i, off


def place(k, slot, c, base):
    i, off = slot_row(k, slot)
    a = i - c + MID + base
    b = k + 8 * off - c + MID + base
    ok = (a >= 0) & (a < BW) & (b >= 0) & (b < BW)
    return a, b, ok


def split(x):
    hi = x.astype(BF16)
    lo = (x - hi.astype(F32)).astype(BF16)
    return hi, lo


def kernel(
    d_ref, h_ref, nb_ref, new_ref, en_ref,
    gat, rel, hal, whi, wlo, xhi, xlo, x2hi, x2lo, sq, mx, rmx, oc, ro, msk,
    gss, grs, rss, rrs, hss, hrs, mss, mrs, oss, ors,
):
    bs = d_ref.shape[-1]
    r = lax.axis_index("row")
    c = lax.axis_index("col")
    up = (lax.rem(r + 1, N_ROW), c)
    down = (lax.rem(r + N_ROW - 1, N_ROW), c)

    def owner(a):
        t = c + 1 + a
        return (lax.rem(r + t // 8 - 1 + N_ROW, N_ROW), lax.rem(t, 8))

    barrier = pltpu.get_barrier_semaphore()
    for a in range(BW):
        if a != MID:
            pl.semaphore_signal(barrier, inc=1, device_id=owner(a), device_id_type=MESH)
    pl.semaphore_signal(barrier, inc=1, device_id=up, device_id_type=MESH)
    pl.semaphore_signal(barrier, inc=1, device_id=down, device_id_type=MESH)

    def rows(a):
        return pl.ds(pl.multiple_of(a * bs, bs), bs)

    def own_slot(i):
        return jnp.where(i <= c, 1, 0)

    col_mine = (8 * r + c - MID + NB + lax.broadcasted_iota(jnp.int32, (16, 16), 0)) % NB
    hit = jnp.where(nb_ref[pl.ds(c, 1), :] == col_mine, 1.0, 0.0).astype(F32)
    msk[0:16, :] = jnp.broadcast_to(jnp.max(hit, axis=1, keepdims=True), (16, bs))
    row_i = lax.broadcasted_iota(jnp.int32, (8, 16), 0)
    col_other = (8 * r + c + NB + jnp.where(row_i > c, 8, -8)) % NB
    hit = jnp.where(nb_ref[...] == col_other, 1.0, 0.0).astype(F32)
    msk[16:24, :] = jnp.broadcast_to(jnp.max(hit, axis=1, keepdims=True), (8, bs))

    def contribute(slot, _):
        i, off = slot_row(c, slot)
        other = off * off
        mine = own_slot(i)
        t = mine + other - 2 * mine * other
        m = msk[pl.ds((1 - other) * (i - c + MID) + other * (16 + i), 1), :]
        gat[c, slot] = d_ref[i, t] * m
        return 0

    lax.fori_loop(0, 8, contribute, 0)
    pl.semaphore_wait(barrier, 16)

    sends = []

    def part(k, p):
        return gat.at[k, pl.ds(HALF * p, HALF)]

    counts = [0, 0]

    def start_forward(p, delta, dim):
        k = class_of(c, delta)
        cp = pltpu.make_async_remote_copy(
            src_ref=part(k, p), dst_ref=part(k, p),
            send_sem=gss.at[p, counts[p]], recv_sem=grs.at[p, delta ^ dim],
            device_id=(r, class_of(c, dim)), device_id_type=MESH,
        )
        counts[p] += 1
        cp.start()
        sends.append(cp)

    order = {0: (1, 2, 4), 1: (1, 4, 2)}

    def dims_after(p, delta):
        o = order[p]
        last = max([o.index(d) for d in o if delta & d], default=-1)
        return o[last + 1:]

    for n in range(3):
        for p in (0, 1):
            start_forward(p, 0, order[p][n])

    def send_h(i, _):
        @pl.when(i != c)
        def _():
            t = 1 - own_slot(i)
            pltpu.make_async_remote_copy(
                src_ref=h_ref.at[i, t], dst_ref=hal.at[i],
                send_sem=hss.at[i], recv_sem=hrs.at[i],
                device_id=(lax.rem(r + jnp.where(i > c, 1, N_ROW - 1), N_ROW), c), device_id_type=MESH,
            ).start()
        return 0

    lax.fori_loop(0, 8, send_h, 0)

    def relay_copy(k, slot, is_up):
        return pltpu.make_async_remote_copy(
            src_ref=gat.at[k, slot], dst_ref=rel.at[k, slot],
            send_sem=rss.at[k, slot], recv_sem=rrs.at[k, slot],
            device_id=(lax.rem(r + jnp.where(is_up, 1, N_ROW - 1), N_ROW), c), device_id_type=MESH,
        )

    def put(x, a, b):
        hi, lo = split(x)
        whi[rows(a), rows(b)] = hi
        wlo[rows(a), rows(b)] = lo
        hi, lo = split(x.T)
        whi[rows(b), rows(a)] = hi
        wlo[rows(b), rows(a)] = lo

    def relay_part(k, p):
        def step(j, _):
            slot = HALF * p + j
            _, _, is_up = place(k, slot, c, -8)
            _, _, is_down = place(k, slot, c, 8)

            @pl.when(is_up | is_down)
            def _():
                relay_copy(k, slot, is_up).start()
            return 0

        lax.fori_loop(0, HALF, step, 0)

    def put_part(k, p):
        def step(j, _):
            slot = HALF * p + j
            a, b, ok = place(k, slot, c, 0)

            @pl.when(ok)
            def _():
                put(gat[k, slot], a, b)
            return 0

        lax.fori_loop(0, HALF, step, 0)

    for p in (0, 1):
        relay_part(c, p)

    zero = jnp.zeros((bs, bs), BF16)
    for g in range(BW // GROUP):
        lo_b, hi_b = max(0, GROUP * g - MID), min(BW - 1, GROUP * g + GROUP - 1 + MID)
        for a in range(GROUP * g, GROUP * g + GROUP):
            for b in range(lo_b, hi_b + 1):
                if abs(a - b) > MID:
                    whi[a * bs:(a + 1) * bs, b * bs:(b + 1) * bs] = zero
                    wlo[a * bs:(a + 1) * bs, b * bs:(b + 1) * bs] = zero
    for p in (0, 1):
        put_part(c, p)

    def arrive(p, delta):
        k = class_of(c, delta)
        pltpu.make_async_remote_copy(
            src_ref=part(k, p), dst_ref=part(k, p),
            send_sem=gss.at[p, 0], recv_sem=grs.at[p, delta],
            device_id=(r, class_of(c, 1)), device_id_type=MESH,
        ).wait_recv()
        for dim in dims_after(p, delta):
            start_forward(p, delta, dim)
        relay_part(k, p)

    events = [(0, 1), (1, 1), (0, 2), (1, 4), (0, 3), (1, 5), (0, 4), (1, 2), (0, 5), (1, 3), (0, 6), (1, 6), (0, 7), (1, 7)]
    pending = None
    for p, delta in events:
        arrive(p, delta)
        if pending is not None:
            put_part(*pending)
        pending = (class_of(c, delta), p)
    put_part(*pending)

    def put_h(x, a):
        hi, lo = split(x * msk[pl.ds(a, 1), :])
        xhi[rows(a), bs:2 * bs] = hi
        xlo[rows(a), bs:2 * bs] = lo

    def h_copy(i):
        return pltpu.make_async_remote_copy(
            src_ref=h_ref.at[i, 0], dst_ref=hal.at[i],
            send_sem=hss.at[i], recv_sem=hrs.at[i],
            device_id=up, device_id_type=MESH,
        )

    def take_h(i, _):
        put_h(h_ref[i, own_slot(i)], i - c + MID)

        @pl.when(i != c)
        def _():
            h_copy(i).wait_recv()
            put_h(hal[i], i - c + jnp.where(i > c, -1, 15))
        return 0

    lax.fori_loop(0, 8, take_h, 0)

    def take_relay(n, _):
        k = n // 8
        slot = n % 8
        a0, b0, below = place(k, slot, c, -8)
        a1, b1, above = place(k, slot, c, 8)

        @pl.when(below | above)
        def _():
            relay_copy(k, slot, below).wait_recv()
            put(rel[k, slot], jnp.where(below, a0, a1), jnp.where(below, b0, b1))
        return 0

    lax.fori_loop(0, 64, take_relay, 0)

    xhi[:, 0:bs] = whi[:, MID * bs:(MID + 1) * bs]
    xlo[:, 0:bs] = wlo[:, MID * bs:(MID + 1) * bs]

    def product(g, vhi, vlo):
        lo_b, hi_b = max(0, GROUP * g - MID), min(BW - 1, GROUP * g + GROUP - 1 + MID)
        rs = slice(GROUP * g * bs, GROUP * (g + 1) * bs)
        ks = slice(lo_b * bs, (hi_b + 1) * bs)
        dot = functools.partial(jnp.dot, preferred_element_type=F32)
        return dot(whi[rs, ks], vhi[ks, :]) + dot(whi[rs, ks], vlo[ks, :]) + dot(wlo[rs, ks], vhi[ks, :])

    def mx_copy(a, back):
        return pltpu.make_async_remote_copy(
            src_ref=mx.at[a], dst_ref=rmx.at[back],
            send_sem=mss.at[a], recv_sem=mrs.at[back],
            device_id=owner(a), device_id_type=MESH,
        )

    for g in range(BW // GROUP):
        y = product(g, xhi, xlo)
        for n in range(GROUP):
            a = GROUP * g + n
            m = msk[a:a + 1, :]
            s = y[n * bs:(n + 1) * bs, 0:bs] * m
            sq[a] = s
            hi, lo = split(s)
            x2hi[a * bs:(a + 1) * bs, 0:bs] = hi
            x2lo[a * bs:(a + 1) * bs, 0:bs] = lo
            mx[a] = y[n * bs:(n + 1) * bs, bs:2 * bs] * m
            if a != MID:
                mx_copy(a, BW - 1 - a).start()

    def put_mx(x, a):
        hi, lo = split(x.T)
        x2hi[rows(a), bs:2 * bs] = hi
        x2lo[rows(a), bs:2 * bs] = lo

    put_mx(mx[MID], MID)
    for a in range(BW):
        if a != MID:
            mx_copy(BW - 1 - a, a).wait_recv()
            put_mx(rmx[a], a)

    def out_copy(a):
        t = c + 1 + a
        return pltpu.make_async_remote_copy(
            src_ref=oc.at[a], dst_ref=ro.at[lax.rem(t, 8)],
            send_sem=oss.at[a], recv_sem=ors.at[lax.rem(t, 8)],
            device_id=(lax.rem(r + t // 8 - 1 + N_ROW, N_ROW), c), device_id_type=MESH,
        )

    for g in range(BW // GROUP):
        y = product(g, x2hi, x2lo)
        for n in range(GROUP):
            a = GROUP * g + n
            m = msk[a:a + 1, :]
            oc[a, 0] = 3.0 * sq[a] - 2.0 * (y[n * bs:(n + 1) * bs, 0:bs] * m)
            oc[a, 1] = y[n * bs:(n + 1) * bs, bs:2 * bs] * m
            if a != MID:
                @pl.when((c + 1 + a < 8) | (c + 1 + a >= 16))
                def _():
                    out_copy(a).start()

    def finish(i, _):
        t = own_slot(i)
        new_ref[i, t] = oc[i - c + MID, 0]
        en_ref[i, t] = oc[i - c + MID, 1]

        @pl.when(i == c)
        def _():
            new_ref[i, 0] = jnp.zeros((bs, bs), F32)
            en_ref[i, 0] = jnp.zeros((bs, bs), F32)

        @pl.when(i != c)
        def _():
            pltpu.make_async_remote_copy(
                src_ref=oc.at[0], dst_ref=ro.at[i],
                send_sem=oss.at[0], recv_sem=ors.at[i],
                device_id=up, device_id_type=MESH,
            ).wait_recv()
            new_ref[i, 1 - t] = ro[i, 0]
            en_ref[i, 1 - t] = ro[i, 1]
        return 0

    lax.fori_loop(0, 8, finish, 0)

    for cp in sends:
        cp.wait_send()

    def sent_h(i, _):
        @pl.when(i != c)
        def _():
            h_copy(i).wait_send()
        return 0

    lax.fori_loop(0, 8, sent_h, 0)

    def sent_relay(n, _):
        k = n // 8
        slot = n % 8
        _, _, is_up = place(k, slot, c, -8)
        _, _, is_down = place(k, slot, c, 8)

        @pl.when(is_up | is_down)
        def _():
            relay_copy(k, slot, is_up).wait_send()
        return 0

    lax.fori_loop(0, 64, sent_relay, 0)
    for a in range(BW):
        if a != MID:
            mx_copy(a, BW - 1 - a).wait_send()

            @pl.when((c + 1 + a < 8) | (c + 1 + a >= 16))
            def _():
                out_copy(a).wait_send()


def body(density, hamiltonian, neighbours):
    bs = density.shape[-1]
    block = (bs, bs)
    wide = (BW * bs, BW * bs)
    tall = (BW * bs, 2 * bs)
    vm = pl.BlockSpec(memory_space=pltpu.VMEM)
    dma = pltpu.SemaphoreType.DMA
    out = jax.ShapeDtypeStruct(density.shape, F32)
    return pl.pallas_call(
        kernel,
        out_shape=(out, out),
        in_specs=[vm] * 3,
        out_specs=(vm, vm),
        scratch_shapes=[
            pltpu.VMEM((8, 8) + block, F32),
            pltpu.VMEM((8, 8) + block, F32),
            pltpu.VMEM((8,) + block, F32),
            pltpu.VMEM(wide, BF16),
            pltpu.VMEM(wide, BF16),
            pltpu.VMEM(tall, BF16),
            pltpu.VMEM(tall, BF16),
            pltpu.VMEM(tall, BF16),
            pltpu.VMEM(tall, BF16),
            pltpu.VMEM((BW,) + block, F32),
            pltpu.VMEM((BW,) + block, F32),
            pltpu.VMEM((BW,) + block, F32),
            pltpu.VMEM((BW, 2) + block, F32),
            pltpu.VMEM((8, 2) + block, F32),
            pltpu.VMEM((24, bs), F32),
            dma((2, 7)), dma((2, 8)),
            dma((8, 8)), dma((8, 8)),
            dma((8,)), dma((8,)),
            dma((BW,)), dma((BW,)),
            dma((BW,)), dma((8,)),
        ],
        compiler_params=pltpu.CompilerParams(
            collective_id=0, has_side_effects=True, vmem_limit_bytes=56 * 2**20
        ),
        cost_estimate=pl.CostEstimate(flops=9 * 10**9, bytes_accessed=4 * 2**20, transcendentals=0),
        name="purify",
    )(density, hamiltonian, neighbours)


def solution(mesh):
    placed = (P("row", "col", None, None), P("row", "col", None, None), P("row", None))
    return jax.shard_map(
        body,
        mesh=mesh,
        in_specs=placed,
        out_specs=(P("row", "col", None, None), P("row", "col", None, None)),
        check_vma=False,
    )
```

```python
import functools
import jax
import jax.numpy as jnp
from jax import lax
from jax.experimental import pallas as pl
from jax.experimental.pallas import tpu as pltpu
from jax.sharding import PartitionSpec as P

MESH = pl.DeviceIdType.MESH
F32 = jnp.float32
BF16 = jnp.bfloat16
R8 = 8
N_ROW = 16
NB = 128
BW = 15
MID = 7
GATHER = tuple(((1, 2, 4), (4, 1, 2), (2, 4, 1))[n % 3] for n in range(8))
SPREAD = ((4, 2, 1), (2, 4, 1), (2, 4, 1), (4, 2, 1), (1, 2, 4), (4, 2, 1), (1, 2, 4), (1, 2, 4))
GROUPS = (0, 4, 1, 3, 2)
GROUP = 3


def class_of(c, delta):
    if delta & 1:
        c = c + 1 - 2 * (c % 2)
    if delta & 2:
        c = c + 2 * (1 - 2 * ((c // 2) % 2))
    if delta & 4:
        c = c % 2 + 6 - 2 * (c // 2)
    return c


def slot_row(k, slot):
    if isinstance(slot, int):
        t = k + (slot - 4 if slot > 4 else slot)
    else:
        t = k + jnp.where(slot > 4, slot - 4, slot)
    wrapped = t >= 8
    i = jnp.where(wrapped, t - 8, t)
    if isinstance(slot, int):
        if slot < 4:
            return i, 0
        return i, jnp.where(wrapped, -1, 0 if slot == 4 else 1)
    return i, jnp.where(wrapped & (slot >= 4), -1, jnp.where(slot > 4, 1, 0))


def limits(k, slot):
    i, off = slot_row(k, slot)
    under, over = jnp.minimum(k, i), jnp.maximum(k, i)
    if not isinstance(off, int):
        under = jnp.where(off == 0, under, jnp.where(off > 0, i, 0))
        over = jnp.where(off == 0, over, jnp.where(off < 0, i, 7))
    return i, off, under, over


def dims_after(o, delta):
    last = max([n for n in range(3) if delta & o[n]], default=-1)
    return o[last + 1:]


def subtree(o, delta):
    found = [delta]
    for d in dims_after(o, delta):
        found += [x | d for x in found]
    return found


def split(x):
    hi = x.astype(BF16)
    lo = (x - hi.astype(F32)).astype(BF16)
    return hi, lo


def kernel(
    d_ref, h_ref, nb_ref, new_ref, en_ref,
    gat, rel, ext, hal, whi, wlo, xhi, xlo, x2s, x2m, sq, mx, rmx, oc, ro, msk,
    gss, grs, rss, rrs, ess, ers, zss, hss, hrs, mss, mrs, oss, ors,
):
    bs = d_ref.shape[-1]
    r = lax.axis_index("row")
    c = lax.axis_index("col")
    above = jnp.where(r == N_ROW - 1, 0, r + 1)
    below = jnp.where(r == 0, N_ROW - 1, r - 1)
    up = (above, c)
    down = (below, c)
    cls = [class_of(c, delta) for delta in range(8)]

    def owner(a):
        t = c + 1 + a
        row = jnp.where(t < 8, below, jnp.where(t < 16, r, above))
        return (row, jnp.where(t < 8, t, jnp.where(t < 16, t - 8, t - 16)))

    barrier = pltpu.get_barrier_semaphore()
    for a in range(BW):
        if a != MID:
            pl.semaphore_signal(barrier, inc=1, device_id=owner(a), device_id_type=MESH)
    pl.semaphore_signal(barrier, inc=1, device_id=up, device_id_type=MESH)
    pl.semaphore_signal(barrier, inc=1, device_id=down, device_id_type=MESH)

    def rows(a):
        return pl.ds(pl.multiple_of(a * bs, bs), bs)

    def own_slot(i):
        return jnp.where(i <= c, 1, 0)

    col_mine = (8 * r + c - MID + NB + lax.broadcasted_iota(jnp.int32, (16, 16), 0)) % NB
    hit = jnp.where(nb_ref[pl.ds(c, 1), :] == col_mine, 1.0, 0.0).astype(F32)
    msk[0:16, :] = jnp.broadcast_to(jnp.max(hit, axis=1, keepdims=True), (16, bs))
    row_i = lax.broadcasted_iota(jnp.int32, (8, 16), 0)
    col_other = (8 * r + c + NB + jnp.where(row_i > c, 8, -8)) % NB
    hit = jnp.where(nb_ref[...] == col_other, 1.0, 0.0).astype(F32)
    msk[16:24, :] = jnp.broadcast_to(jnp.max(hit, axis=1, keepdims=True), (8, bs))

    def contribute(slot, _):
        i, off = slot_row(c, slot)
        mine = own_slot(i)
        t = jnp.where(off == 0, mine, 1 - mine)
        m = msk[pl.ds(jnp.where(off == 0, i - c + MID, 16 + i), 1), :]
        gat[c, slot] = d_ref[i, t] * m
        return 0

    lax.fori_loop(0, 8, contribute, 0)
    pl.semaphore_wait(barrier, 16)

    sends = []
    counts = [0] * 8
    in_x_half = (r // 2) % 4
    low = 1 - lax.rem(r, 2)
    crossing = jnp.where(in_x_half == jnp.where(low == 1, 0, 3), 1, 0)

    def start_forward(slot, delta, dim):
        k = cls[delta]
        cp = pltpu.make_async_remote_copy(
            src_ref=gat.at[k, slot], dst_ref=gat.at[k, slot],
            send_sem=gss.at[slot, counts[slot]], recv_sem=grs.at[slot, delta ^ dim],
            device_id=(r, cls[dim]), device_id_type=MESH,
        )
        counts[slot] += 1
        cp.start()
        sends.append(cp)

    for slot in range(8):
        start_forward(slot, 0, GATHER[slot][0])

    beyond_r = jnp.where(low == 1, below, above)

    def reach(k, slot, is_low):
        i, off, under, over = limits(k, slot)
        found = jnp.where(is_low == 1, under, 7 - over)
        return jnp.where((crossing == 1) | (off != 0), found, 0)

    def cross_copy(slot):
        return pltpu.make_async_remote_copy(
            src_ref=gat.at[c, slot], dst_ref=ext.at[c, slot],
            send_sem=zss.at[slot], recv_sem=ers.at[c, slot],
            device_id=(beyond_r, c), device_id_type=MESH,
        )

    for slot in range(8):
        @pl.when(reach(c, slot, 1 - low) > 0)
        def _():
            cross_copy(slot).start()

    for slot in range(8):
        start_forward(slot, 0, GATHER[slot][1])

    dist = [jnp.where(low == 1, k, 7 - k) for k in cls]
    reached = {}

    def neediest(o, delta, dim):
        nodes = frozenset(delta ^ x for x in subtree(o, delta | dim))
        if nodes not in reached:
            reached[nodes] = functools.reduce(jnp.minimum, [dist[x] for x in sorted(nodes)])
        return reached[nodes]

    mine = dist[0]
    base = jnp.where(low == 1, -8, 8)
    def spread_copy(k, slot, dim, n):
        return pltpu.make_async_remote_copy(
            src_ref=ext.at[k, slot], dst_ref=ext.at[k, slot],
            send_sem=ess.at[k, slot, n], recv_sem=ers.at[k, slot],
            device_id=(r, cls[dim]), device_id_type=MESH,
        )

    onward = {}

    def spread(pick):
        for slot in range(8):
            o = SPREAD[slot]
            delta = pick(o)
            k = cls[delta]
            here = neediest(o, delta, 0)
            if (o, delta) not in onward:
                onward[o, delta] = [(dim, neediest(o, delta, dim)) for dim in dims_after(o, delta)]
            need = reach(k, slot, low)

            @pl.when(here < need)
            def _():
                spread_copy(k, slot, 1, 0).wait_recv()
                for n, (dim, v) in enumerate(onward[o, delta]):
                    @pl.when(v < need)
                    def _():
                        spread_copy(k, slot, dim, n).start()

    def spread_sent(slot, delta):
        o = SPREAD[slot]
        k = cls[delta]
        need = reach(k, slot, low)
        for n, (dim, v) in enumerate(onward[o, delta]):
            @pl.when((neediest(o, delta, 0) < need) & (v < need))
            def _():
                spread_copy(k, slot, dim, n).wait_send()

    def class_at(orders, pick, slot):
        deltas = [pick(o) for o in orders]
        k = cls[deltas[0]]
        for delta in sorted(set(deltas) - {deltas[0]}):
            hit = functools.reduce(jnp.logical_or, [slot == n for n in range(8) if deltas[n] == delta])
            k = jnp.where(hit, cls[delta], k)
        return k

    def put_spread(pick):
        def step(slot, _):
            k = class_at(SPREAD, pick, slot)

            @pl.when(mine < reach(k, slot, low))
            def _():
                i, off = slot_row(k, slot)
                put(ext[k, slot], i - c + MID + base, k + 8 * off - c + MID + base)
            return 0

        lax.fori_loop(0, 8, step, 0)

    def send_h(i, _):
        @pl.when(i != c)
        def _():
            t = 1 - own_slot(i)
            pltpu.make_async_remote_copy(
                src_ref=h_ref.at[i, t], dst_ref=hal.at[i],
                send_sem=hss.at[i], recv_sem=hrs.at[i],
                device_id=(jnp.where(i > c, above, below), c), device_id_type=MESH,
            ).start()
        return 0

    lax.fori_loop(0, 8, send_h, 0)

    def relayed(k, slot, inner_up):
        i, off, under, over = limits(k, slot)
        plain = (off == 0) & (crossing == 0)
        return i, off, (c < under) & (plain | (inner_up == 1)), (c > over) & (plain | (inner_up == 0))

    def relay_copy(k, slot, is_up):
        return pltpu.make_async_remote_copy(
            src_ref=gat.at[k, slot], dst_ref=rel.at[k, slot],
            send_sem=rss.at[k, slot], recv_sem=rrs.at[k, slot],
            device_id=(jnp.where(is_up, above, below), c), device_id_type=MESH,
        )

    def put(x, a, b):
        hi, lo = split(x)
        whi[rows(a), rows(b)] = hi
        wlo[rows(a), rows(b)] = lo
        hi, lo = split(x.T)
        whi[rows(b), rows(a)] = hi
        wlo[rows(b), rows(a)] = lo

    def relay(pick):
        for slot in range(8):
            k = cls[pick(GATHER[slot])]
            _, _, is_up, is_down = relayed(k, slot, low)

            @pl.when(is_up | is_down)
            def _():
                relay_copy(k, slot, is_up).start()

    def put_own(pick):
        def step(slot, _):
            k = class_at(GATHER, pick, slot)
            i, off = slot_row(k, slot)
            b = k + 8 * off - c + MID

            @pl.when((b >= 0) & (b < BW))
            def _():
                put(gat[k, slot], i - c + MID, b)
            return 0

        lax.fori_loop(0, 8, step, 0)

    def put_relayed(pick):
        def step(slot, _):
            k = class_at(GATHER, pick, slot)
            i, off, from_below, from_above = relayed(k, slot, 1 - low)

            @pl.when(from_below | from_above)
            def _():
                relay_copy(k, slot, from_below).wait_recv()
                shift = jnp.where(from_below, -8, 8) - c + MID
                put(rel[k, slot], i + shift, k + 8 * off + shift)
            return 0

        lax.fori_loop(0, 8, step, 0)

    w0 = lambda o: 0
    w1 = lambda o: o[0]
    w2 = lambda o: o[1]
    w3 = lambda o: o[2]
    w12 = lambda o: o[0] | o[1]
    w13 = lambda o: o[0] | o[2]
    w23 = lambda o: o[1] | o[2]
    w123 = lambda o: 7
    relay(w0)

    zero = jnp.zeros((bs, bs), BF16)
    for g in range(BW // GROUP):
        lo_b, hi_b = max(0, GROUP * g - MID), min(BW - 1, GROUP * g + GROUP - 1 + MID)
        for a in range(GROUP * g, GROUP * g + GROUP):
            for b in range(lo_b, hi_b + 1):
                if abs(a - b) > MID:
                    whi[a * bs:(a + 1) * bs, b * bs:(b + 1) * bs] = zero
                    wlo[a * bs:(a + 1) * bs, b * bs:(b + 1) * bs] = zero
    put_own(w0)

    def arrive(slot, delta):
        k = cls[delta]
        pltpu.make_async_remote_copy(
            src_ref=gat.at[k, slot], dst_ref=gat.at[k, slot],
            send_sem=gss.at[slot, 0], recv_sem=grs.at[slot, delta],
            device_id=(r, cls[1]), device_id_type=MESH,
        ).wait_recv()

    def wave(pick, dims):
        for slot in range(8):
            o = GATHER[slot]
            arrive(slot, pick(o))
            for n in dims:
                start_forward(slot, pick(o), o[n])

    wave(w1, (1,))
    for slot in range(8):
        start_forward(slot, 0, GATHER[slot][2])
        start_forward(slot, GATHER[slot][0], GATHER[slot][2])
    relay(w1)
    spread(w0)
    put_relayed(w0)
    put_own(w1)
    wave(w2, (2,))
    relay(w2)
    spread(w1)
    put_relayed(w1)
    wave(w12, (2,))
    relay(w12)
    spread(w2)
    put_own(w2)
    put_spread(w0)
    spread(w12)
    put_spread(w1)
    put_own(w12)
    put_relayed(w2)
    wave(w3, ())
    relay(w3)
    put_own(w3)
    put_relayed(w12)
    put_spread(w2)
    wave(w13, ())
    relay(w13)
    put_own(w13)
    put_spread(w12)
    put_relayed(w3)
    spread(w3)
    put_spread(w3)
    spread(w13)
    put_spread(w13)
    wave(w23, ())
    relay(w23)
    put_own(w23)
    put_relayed(w13)
    wave(w123, ())
    relay(w123)
    put_own(w123)
    spread(w23)
    put_spread(w23)
    put_relayed(w23)
    spread(w123)
    put_spread(w123)
    put_relayed(w123)

    def put_h(x, a):
        hi, lo = split(x * msk[pl.ds(a, 1), :])
        xhi[rows(a), bs:2 * bs] = hi
        xlo[rows(a), bs:2 * bs] = lo

    def h_copy(i):
        return pltpu.make_async_remote_copy(
            src_ref=h_ref.at[i, 0], dst_ref=hal.at[i],
            send_sem=hss.at[i], recv_sem=hrs.at[i],
            device_id=up, device_id_type=MESH,
        )

    def take_h(i, _):
        put_h(h_ref[i, own_slot(i)], i - c + MID)

        @pl.when(i != c)
        def _():
            h_copy(i).wait_recv()
            put_h(hal[i], i - c + jnp.where(i > c, -1, 15))
        return 0

    lax.fori_loop(0, 8, take_h, 0)

    xhi[:, 0:bs] = whi[:, MID * bs:(MID + 1) * bs]
    xlo[:, 0:bs] = wlo[:, MID * bs:(MID + 1) * bs]

    def product(g, vhi, vlo):
        lo_b, hi_b = max(0, GROUP * g - MID), min(BW - 1, GROUP * g + GROUP - 1 + MID)
        rs = slice(GROUP * g * bs, GROUP * (g + 1) * bs)
        ks = slice(lo_b * bs, (hi_b + 1) * bs)
        dot = functools.partial(jnp.dot, preferred_element_type=F32)
        return dot(whi[rs, ks], vhi[ks, :]) + dot(whi[rs, ks], vlo[ks, :]) + dot(wlo[rs, ks], vhi[ks, :])

    def mx_copy(a, back):
        return pltpu.make_async_remote_copy(
            src_ref=mx.at[a], dst_ref=rmx.at[back],
            send_sem=mss.at[a], recv_sem=mrs.at[back],
            device_id=owner(a), device_id_type=MESH,
        )

    for g in GROUPS:
        y = product(g, xhi, xlo)
        for n in range(GROUP):
            a = GROUP * g + n
            m = msk[a:a + 1, :]
            mx[a] = y[n * bs:(n + 1) * bs, bs:2 * bs] * m
            if a != MID:
                mx_copy(a, BW - 1 - a).start()
            x = y[n * bs:(n + 1) * bs, 0:bs] * m
            sq[a] = x
            hi, lo = split(x)
            x2s[a * bs:(a + 1) * bs, 0:bs] = hi
            x2s[a * bs:(a + 1) * bs, bs:2 * bs] = lo

    def half_product(g, v):
        lo_b, hi_b = max(0, GROUP * g - MID), min(BW - 1, GROUP * g + GROUP - 1 + MID)
        rs = slice(GROUP * g * bs, GROUP * (g + 1) * bs)
        ks = slice(lo_b * bs, (hi_b + 1) * bs)
        dot = functools.partial(jnp.dot, preferred_element_type=F32)
        y = dot(whi[rs, ks], v[ks, :])
        return y[:, 0:bs] + y[:, bs:2 * bs] + dot(wlo[rs, ks], v[ks, 0:bs])

    def out_copy(which, a):
        row, i = owner(a)
        return pltpu.make_async_remote_copy(
            src_ref=oc.at[which, a], dst_ref=ro.at[which, i],
            send_sem=oss.at[which, a], recv_sem=ors.at[which, i],
            device_id=(row, c), device_id_type=MESH,
        )

    def leaves(a):
        return (c + 1 + a < 8) | (c + 1 + a >= 16)

    def send_out(which, a):
        if a != MID:
            @pl.when(leaves(a))
            def _():
                out_copy(which, a).start()

    for g in GROUPS:
        y = half_product(g, x2s)
        for n in range(GROUP):
            a = GROUP * g + n
            oc[0, a] = 3.0 * sq[a] - 2.0 * (y[n * bs:(n + 1) * bs, :] * msk[a:a + 1, :])
            send_out(0, a)

    def put_mx(x, a):
        hi, lo = split(x.T)
        x2m[rows(a), 0:bs] = hi
        x2m[rows(a), bs:2 * bs] = lo

    put_mx(mx[MID], MID)
    for a in range(BW):
        if a != MID:
            mx_copy(BW - 1 - a, a).wait_recv()
            put_mx(rmx[a], a)

    for g in GROUPS:
        y = half_product(g, x2m)
        for n in range(GROUP):
            a = GROUP * g + n
            oc[1, a] = y[n * bs:(n + 1) * bs, :] * msk[a:a + 1, :]
            send_out(1, a)

    def finish(which, ref):
        def step(i, _):
            t = own_slot(i)
            ref[i, t] = oc[which, i - c + MID]

            @pl.when(i == c)
            def _():
                ref[i, 0] = jnp.zeros((bs, bs), F32)

            @pl.when(i != c)
            def _():
                pltpu.make_async_remote_copy(
                    src_ref=oc.at[which, 0], dst_ref=ro.at[which, i],
                    send_sem=oss.at[which, 0], recv_sem=ors.at[which, i],
                    device_id=up, device_id_type=MESH,
                ).wait_recv()
                ref[i, 1 - t] = ro[which, i]
            return 0

        lax.fori_loop(0, 8, step, 0)

    finish(0, new_ref)
    finish(1, en_ref)

    for cp in sends:
        cp.wait_send()

    def sent_h(i, _):
        @pl.when(i != c)
        def _():
            h_copy(i).wait_send()
        return 0

    lax.fori_loop(0, 8, sent_h, 0)

    def sent_relay(n, _):
        k = n // 8
        slot = n % 8
        _, _, is_up, is_down = relayed(k, slot, low)

        @pl.when(is_up | is_down)
        def _():
            relay_copy(k, slot, is_up).wait_send()
        return 0

    lax.fori_loop(0, 64, sent_relay, 0)
    for a in range(BW):
        if a != MID:
            mx_copy(a, BW - 1 - a).wait_send()

            @pl.when(leaves(a))
            def _():
                for which in (0, 1):
                    out_copy(which, a).wait_send()

    def cross_sent(slot, _):
        @pl.when(reach(c, slot, 1 - low) > 0)
        def _():
            cross_copy(slot).wait_send()
        return 0

    lax.fori_loop(0, 8, cross_sent, 0)
    for slot in range(8):
        for delta in range(8):
            spread_sent(slot, delta)


def body(density, hamiltonian, neighbours):
    bs = density.shape[-1]
    block = (bs, bs)
    wide = (BW * bs, BW * bs)
    tall = (BW * bs, 2 * bs)
    vm = pl.BlockSpec(memory_space=pltpu.VMEM)
    dma = pltpu.SemaphoreType.DMA
    out = jax.ShapeDtypeStruct(density.shape, F32)
    return pl.pallas_call(
        kernel,
        out_shape=(out, out),
        in_specs=[vm] * 3,
        out_specs=(vm, vm),
        scratch_shapes=[
            pltpu.VMEM((8, 8) + block, F32),
            pltpu.VMEM((8, 8) + block, F32),
            pltpu.VMEM((8, 8) + block, F32),
            pltpu.VMEM((8,) + block, F32),
            pltpu.VMEM(wide, BF16),
            pltpu.VMEM(wide, BF16),
            pltpu.VMEM(tall, BF16),
            pltpu.VMEM(tall, BF16),
            pltpu.VMEM(tall, BF16),
            pltpu.VMEM(tall, BF16),
            pltpu.VMEM((BW,) + block, F32),
            pltpu.VMEM((BW,) + block, F32),
            pltpu.VMEM((BW,) + block, F32),
            pltpu.VMEM((2, BW) + block, F32),
            pltpu.VMEM((2, 8) + block, F32),
            pltpu.VMEM((24, bs), F32),
            dma((8, 7)), dma((8, 8)),
            dma((8, 8)), dma((8, 8)),
            dma((8, 8, 3)), dma((8, 8)), dma((8,)),
            dma((8,)), dma((8,)),
            dma((BW,)), dma((BW,)),
            dma((2, BW)), dma((2, 8)),
        ],
        compiler_params=pltpu.CompilerParams(
            collective_id=0, has_side_effects=True, vmem_limit_bytes=44 * 2**20
        ),
        cost_estimate=pl.CostEstimate(flops=9 * 10**9, bytes_accessed=4 * 2**20, transcendentals=0),
        name="purify",
    )(density, hamiltonian, neighbours)


def solution(mesh):
    placed = (P("row", "col", None, None), P("row", "col", None, None), P("row", None))
    return jax.shard_map(
        body,
        mesh=mesh,
        in_specs=placed,
        out_specs=(P("row", "col", None, None), P("row", "col", None, None)),
        check_vma=False,
    )
```

```python
import functools
import jax
import jax.numpy as jnp
from jax import lax
from jax.experimental import pallas as pl
from jax.experimental.pallas import tpu as pltpu
from jax.sharding import PartitionSpec as P

MESH = pl.DeviceIdType.MESH
F32 = jnp.float32
BF16 = jnp.bfloat16
R8 = 8
N_ROW = 16
NB = 128
BW = 15
MID = 7
GATHER = tuple(((1, 2, 4), (4, 1, 2), (2, 4, 1))[n % 3] for n in range(8))
SPREAD = ((4, 2, 1), (2, 4, 1), (2, 4, 1), (4, 2, 1), (1, 2, 4), (4, 2, 1), (1, 2, 4), (1, 2, 4))
PAIRS = (6, 8, 4, 10, 2, 12, 0, 14)
LEAVE = (0, 14, 1, 13, 2, 12, 3, 11, 4, 10, 5, 9, 6, 8, 7)


def class_of(c, delta):
    if delta & 1:
        c = c + 1 - 2 * (c % 2)
    if delta & 2:
        c = c + 2 * (1 - 2 * ((c // 2) % 2))
    if delta & 4:
        c = c % 2 + 6 - 2 * (c // 2)
    return c


def slot_row(k, slot):
    if isinstance(slot, int):
        t = k + (slot - 4 if slot > 4 else slot)
    else:
        t = k + jnp.where(slot > 4, slot - 4, slot)
    wrapped = t >= 8
    i = jnp.where(wrapped, t - 8, t)
    if isinstance(slot, int):
        if slot < 4:
            return i, 0
        return i, jnp.where(wrapped, -1, 0 if slot == 4 else 1)
    return i, jnp.where(wrapped & (slot >= 4), -1, jnp.where(slot > 4, 1, 0))


def limits(k, slot):
    i, off = slot_row(k, slot)
    under, over = jnp.minimum(k, i), jnp.maximum(k, i)
    if not isinstance(off, int):
        under = jnp.where(off == 0, under, jnp.where(off > 0, i, 0))
        over = jnp.where(off == 0, over, jnp.where(off < 0, i, 7))
    return i, off, under, over


def dims_after(o, delta):
    last = max([n for n in range(3) if delta & o[n]], default=-1)
    return o[last + 1:]


def subtree(o, delta):
    found = [delta]
    for d in dims_after(o, delta):
        found += [x | d for x in found]
    return found


def split(x):
    hi = x.astype(BF16)
    lo = (x - hi.astype(F32)).astype(BF16)
    return hi, lo


def kernel(
    d_hbm, h_hbm, nb_hbm, new_ref, en_ref,
    d_ref, h_ref, nb_ref, isem,
    gat, rel, ext, hal, whi, wlo, xp, xh, x2s, x2m, sq, mx, rmx, oc, ro, msk,
    gss, grs, rss, rrs, ess, ers, zss, hss, hrs, mss, mrs, oss, ors,
):
    bs = d_ref.shape[-1]
    fetch = [
        pltpu.make_async_copy(src, dst, isem.at[n])
        for n, (src, dst) in enumerate(((nb_hbm, nb_ref), (d_hbm, d_ref), (h_hbm, h_ref)))
    ]
    for cp in fetch:
        cp.start()
    r = lax.axis_index("row")
    c = lax.axis_index("col")
    above = jnp.where(r == N_ROW - 1, 0, r + 1)
    below = jnp.where(r == 0, N_ROW - 1, r - 1)
    up = (above, c)
    down = (below, c)
    cls = [class_of(c, delta) for delta in range(8)]

    def owner(a):
        t = c + 1 + a
        row = jnp.where(t < 8, below, jnp.where(t < 16, r, above))
        return (row, jnp.where(t < 8, t, jnp.where(t < 16, t - 8, t - 16)))

    barrier = pltpu.get_barrier_semaphore()
    for a in range(BW):
        if a != MID:
            pl.semaphore_signal(barrier, inc=1, device_id=owner(a), device_id_type=MESH)
    pl.semaphore_signal(barrier, inc=1, device_id=up, device_id_type=MESH)
    pl.semaphore_signal(barrier, inc=1, device_id=down, device_id_type=MESH)

    def rows(a):
        return pl.ds(pl.multiple_of(a * bs, bs), bs)

    def own_slot(i):
        return jnp.where(i <= c, 1, 0)

    fetch[0].wait()
    col_mine = (8 * r + c - MID + NB + lax.broadcasted_iota(jnp.int32, (16, 16), 0)) % NB
    hit = jnp.where(nb_ref[pl.ds(c, 1), :] == col_mine, 1.0, 0.0).astype(F32)
    msk[0:16, :] = jnp.broadcast_to(jnp.max(hit, axis=1, keepdims=True), (16, bs))
    row_i = lax.broadcasted_iota(jnp.int32, (8, 16), 0)
    col_other = (8 * r + c + NB + jnp.where(row_i > c, 8, -8)) % NB
    hit = jnp.where(nb_ref[...] == col_other, 1.0, 0.0).astype(F32)
    msk[16:24, :] = jnp.broadcast_to(jnp.max(hit, axis=1, keepdims=True), (8, bs))

    def contribute(slot, _):
        i, off = slot_row(c, slot)
        mine = own_slot(i)
        t = jnp.where(off == 0, mine, 1 - mine)
        m = msk[pl.ds(jnp.where(off == 0, i - c + MID, 16 + i), 1), :]
        gat[c, slot] = d_ref[i, t] * m
        return 0

    fetch[1].wait()
    lax.fori_loop(0, 8, contribute, 0)
    pl.semaphore_wait(barrier, 16)

    sends = []
    counts = [0] * 8
    in_x_half = (r // 2) % 4
    low = 1 - lax.rem(r, 2)
    crossing = jnp.where(in_x_half == jnp.where(low == 1, 0, 3), 1, 0)

    def start_forward(slot, delta, dim):
        k = cls[delta]
        cp = pltpu.make_async_remote_copy(
            src_ref=gat.at[k, slot], dst_ref=gat.at[k, slot],
            send_sem=gss.at[slot, counts[slot]], recv_sem=grs.at[slot, delta ^ dim],
            device_id=(r, cls[dim]), device_id_type=MESH,
        )
        counts[slot] += 1
        cp.start()
        sends.append(cp)

    for slot in range(8):
        start_forward(slot, 0, GATHER[slot][0])

    beyond_r = jnp.where(low == 1, below, above)

    def reach(k, slot, is_low):
        i, off, under, over = limits(k, slot)
        found = jnp.where(is_low == 1, under, 7 - over)
        return jnp.where((crossing == 1) | (off != 0), found, 0)

    def cross_copy(slot):
        return pltpu.make_async_remote_copy(
            src_ref=gat.at[c, slot], dst_ref=ext.at[c, slot],
            send_sem=zss.at[slot], recv_sem=ers.at[c, slot],
            device_id=(beyond_r, c), device_id_type=MESH,
        )

    for slot in range(8):
        @pl.when(reach(c, slot, 1 - low) > 0)
        def _():
            cross_copy(slot).start()

    for slot in range(8):
        start_forward(slot, 0, GATHER[slot][1])

    dist = [jnp.where(low == 1, k, 7 - k) for k in cls]
    reached = {}

    def neediest(o, delta, dim):
        nodes = frozenset(delta ^ x for x in subtree(o, delta | dim))
        if nodes not in reached:
            reached[nodes] = functools.reduce(jnp.minimum, [dist[x] for x in sorted(nodes)])
        return reached[nodes]

    mine = dist[0]
    base = jnp.where(low == 1, -8, 8)
    def spread_copy(k, slot, dim, n):
        return pltpu.make_async_remote_copy(
            src_ref=ext.at[k, slot], dst_ref=ext.at[k, slot],
            send_sem=ess.at[k, slot, n], recv_sem=ers.at[k, slot],
            device_id=(r, cls[dim]), device_id_type=MESH,
        )

    onward = {}

    def spread(pick, slots=range(8)):
        for slot in slots:
            o = SPREAD[slot]
            delta = pick(o)
            k = cls[delta]
            here = neediest(o, delta, 0)
            if (o, delta) not in onward:
                onward[o, delta] = [(dim, neediest(o, delta, dim)) for dim in dims_after(o, delta)]
            need = reach(k, slot, low)

            @pl.when(here < need)
            def _():
                spread_copy(k, slot, 1, 0).wait_recv()
                for n, (dim, v) in enumerate(onward[o, delta]):
                    @pl.when(v < need)
                    def _():
                        spread_copy(k, slot, dim, n).start()

    def spread_sent(slot, delta):
        o = SPREAD[slot]
        k = cls[delta]
        need = reach(k, slot, low)
        for n, (dim, v) in enumerate(onward[o, delta]):
            @pl.when((neediest(o, delta, 0) < need) & (v < need))
            def _():
                spread_copy(k, slot, dim, n).wait_send()

    def class_at(orders, pick, slot):
        deltas = [pick(o) for o in orders]
        k = cls[deltas[0]]
        for delta in sorted(set(deltas) - {deltas[0]}):
            hit = functools.reduce(jnp.logical_or, [slot == n for n in range(8) if deltas[n] == delta])
            k = jnp.where(hit, cls[delta], k)
        return k

    def put_spread(pick, slots=range(8)):
        def step(slot, _):
            k = class_at(SPREAD, pick, slot)

            @pl.when(mine < reach(k, slot, low))
            def _():
                i, off = slot_row(k, slot)
                put(ext[k, slot], i - c + MID + base, k + 8 * off - c + MID + base)
            return 0

        lax.fori_loop(slots[0], slots[-1] + 1, step, 0)

    def send_h(i, _):
        @pl.when(i != c)
        def _():
            t = 1 - own_slot(i)
            pltpu.make_async_remote_copy(
                src_ref=h_ref.at[i, t], dst_ref=hal.at[i],
                send_sem=hss.at[i], recv_sem=hrs.at[i],
                device_id=(jnp.where(i > c, above, below), c), device_id_type=MESH,
            ).start()
        return 0

    fetch[2].wait()
    lax.fori_loop(0, 8, send_h, 0)

    def relayed(k, slot, inner_up):
        i, off, under, over = limits(k, slot)
        plain = (off == 0) & (crossing == 0)
        return i, off, (c < under) & (plain | (inner_up == 1)), (c > over) & (plain | (inner_up == 0))

    def relay_copy(k, slot, is_up):
        return pltpu.make_async_remote_copy(
            src_ref=gat.at[k, slot], dst_ref=rel.at[k, slot],
            send_sem=rss.at[k, slot], recv_sem=rrs.at[k, slot],
            device_id=(jnp.where(is_up, above, below), c), device_id_type=MESH,
        )

    def put(x, a, b):
        hi, lo = split(x)
        whi[rows(a), rows(b)] = hi
        wlo[rows(a), rows(b)] = lo
        whi[rows(b), rows(a)] = hi.T
        wlo[rows(b), rows(a)] = lo.T

    def relay(pick):
        for slot in range(8):
            k = cls[pick(GATHER[slot])]
            _, _, is_up, is_down = relayed(k, slot, low)

            @pl.when(is_up | is_down)
            def _():
                relay_copy(k, slot, is_up).start()

    def put_own(pick):
        def step(slot, _):
            k = class_at(GATHER, pick, slot)
            i, off = slot_row(k, slot)
            b = k + 8 * off - c + MID

            @pl.when((b >= 0) & (b < BW))
            def _():
                put(gat[k, slot], i - c + MID, b)
            return 0

        lax.fori_loop(0, 8, step, 0)

    def put_relayed(pick, inner=True, outer=True):
        def step(slot, _):
            k = class_at(GATHER, pick, slot)
            i, off, from_below, from_above = relayed(k, slot, 1 - low)
            if not outer:
                from_below, from_above = from_below & (low == 0), from_above & (low == 1)
            if not inner:
                from_below, from_above = from_below & (low == 1), from_above & (low == 0)

            @pl.when(from_below | from_above)
            def _():
                relay_copy(k, slot, from_below).wait_recv()
                shift = jnp.where(from_below, -8, 8) - c + MID
                put(rel[k, slot], i + shift, k + 8 * off + shift)
            return 0

        lax.fori_loop(0, 8, step, 0)

    w0 = lambda o: 0
    w1 = lambda o: o[0]
    w2 = lambda o: o[1]
    w3 = lambda o: o[2]
    w12 = lambda o: o[0] | o[1]
    w13 = lambda o: o[0] | o[2]
    w23 = lambda o: o[1] | o[2]
    w123 = lambda o: 7
    relay(w0)

    zero = jnp.zeros((bs, bs), BF16)
    for b in range(0, BW, 2):
        b1 = min(b + 1, BW - 1)
        for a in range(max(0, b - MID), min(BW - 1, b1 + MID) + 1):
            for q in (b, b1):
                if abs(a - q) > MID:
                    whi[a * bs:(a + 1) * bs, q * bs:(q + 1) * bs] = zero
                    wlo[a * bs:(a + 1) * bs, q * bs:(q + 1) * bs] = zero
    put_own(w0)

    def arrive(slot, delta):
        k = cls[delta]
        pltpu.make_async_remote_copy(
            src_ref=gat.at[k, slot], dst_ref=gat.at[k, slot],
            send_sem=gss.at[slot, 0], recv_sem=grs.at[slot, delta],
            device_id=(r, cls[1]), device_id_type=MESH,
        ).wait_recv()

    def wave(pick, dims):
        for slot in range(8):
            o = GATHER[slot]
            arrive(slot, pick(o))
            for n in dims:
                start_forward(slot, pick(o), o[n])

    wave(w1, (1,))
    for slot in range(8):
        start_forward(slot, 0, GATHER[slot][2])
        start_forward(slot, GATHER[slot][0], GATHER[slot][2])
    relay(w1)
    spread(w0)
    put_relayed(w0)
    put_own(w1)
    wave(w2, (2,))
    relay(w2)
    spread(w1)
    put_relayed(w1)
    wave(w12, (2,))
    relay(w12)
    spread(w2)
    put_own(w2)
    put_spread(w0)
    spread(w12)
    put_spread(w1)
    put_own(w12)
    put_relayed(w2)
    diag = range(0, 4)
    rest = range(4, 8)
    wave(w3, ())
    relay(w3)
    put_own(w3)
    put_relayed(w12, outer=False)
    put_spread(w2)
    wave(w13, ())
    relay(w13)
    put_own(w13)
    put_spread(w12)
    put_relayed(w3, outer=False)
    for w in (w3, w13):
        spread(w, rest)
        put_spread(w, rest)
    wave(w23, ())
    relay(w23)
    put_own(w23)
    put_relayed(w13, outer=False)
    wave(w123, ())
    relay(w123)
    put_own(w123)
    put_relayed(w23, outer=False)
    for w in (w23, w123):
        spread(w, rest)
        put_spread(w, rest)
    put_relayed(w123, outer=False)

    def outer_diagonal():
        for w in (w12, w3, w13):
            put_relayed(w, inner=False)
        for w in (w3, w13, w23, w123):
            spread(w, diag)
            put_spread(w, diag)
        for w in (w23, w123):
            put_relayed(w, inner=False)

    def put_h(x, a):
        hi, lo = split(x * msk[pl.ds(a, 1), :])
        xh[rows(a), 0:bs] = hi
        xh[rows(a), bs:2 * bs] = lo

    def h_copy(i):
        return pltpu.make_async_remote_copy(
            src_ref=h_ref.at[i, 0], dst_ref=hal.at[i],
            send_sem=hss.at[i], recv_sem=hrs.at[i],
            device_id=up, device_id_type=MESH,
        )

    def take_h(i, _):
        put_h(h_ref[i, own_slot(i)], i - c + MID)

        @pl.when(i != c)
        def _():
            h_copy(i).wait_recv()
            put_h(hal[i], i - c + jnp.where(i > c, -1, 15))
        return 0

    lax.fori_loop(0, 8, take_h, 0)


    dot = functools.partial(jnp.dot, preferred_element_type=F32)

    def band(a):
        lo_b, hi_b = max(0, a - MID), min(BW - 1, a + MID)
        return slice(a * bs, (a + 1) * bs), slice(lo_b * bs, (hi_b + 1) * bs)

    def mx_copy(a, back):
        return pltpu.make_async_remote_copy(
            src_ref=mx.at[a], dst_ref=rmx.at[back],
            send_sem=mss.at[a], recv_sem=mrs.at[back],
            device_id=owner(a), device_id_type=MESH,
        )

    def half(a, v):
        rs, ks = band(a)
        y = dot(whi[rs, ks], v[ks, :])
        return y[:, 0:bs] + y[:, bs:2 * bs] + dot(wlo[rs, ks], v[ks, 0:bs])

    def first_product(some):
        for a in some:
            mx[a] = half(a, xh) * msk[a:a + 1, :]
            if a != MID:
                mx_copy(a, BW - 1 - a).start()

    @pl.when(low == 1)
    def _():
        first_product(range(BW - 1, MID - 1, -1))

    @pl.when(low == 0)
    def _():
        first_product(range(0, MID + 1))

    outer_diagonal()

    @pl.when(low == 1)
    def _():
        first_product(range(MID - 1, -1, -1))

    @pl.when(low == 0)
    def _():
        first_product(range(MID + 1, BW))

    xp[:, 0:bs] = whi[:, MID * bs:(MID + 1) * bs]
    xp[:, bs:2 * bs] = wlo[:, MID * bs:(MID + 1) * bs]
    for a in LEAVE:
        x = half(a, xp) * msk[a:a + 1, :]
        sq[a] = x
        hi, lo = split(x)
        x2s[a * bs:(a + 1) * bs, 0:bs] = hi
        x2s[a * bs:(a + 1) * bs, bs:2 * bs] = lo

    def out_copy(which, a):
        row, i = owner(a)
        return pltpu.make_async_remote_copy(
            src_ref=oc.at[which, a], dst_ref=ro.at[which, i],
            send_sem=oss.at[which, a], recv_sem=ors.at[which, i],
            device_id=(row, c), device_id_type=MESH,
        )

    def leaves(a):
        return (c + 1 + a < 8) | (c + 1 + a >= 16)

    def send_out(which, a):
        if a != MID:
            @pl.when(leaves(a))
            def _():
                out_copy(which, a).start()

    for a in LEAVE:
        y = half(a, x2s)
        oc[0, a] = 3.0 * sq[a] - 2.0 * (y * msk[a:a + 1, :])
        send_out(0, a)

    def put_mx(x, a):
        hi, lo = split(x)
        x2m[rows(a), 0:bs] = hi.T
        x2m[rows(a), bs:2 * bs] = lo.T

    put_mx(mx[MID], MID)
    touched = set()
    for b in PAIRS:
        b1 = min(b + 1, BW - 1)
        for a in range(b, b1 + 1):
            if a != MID:
                mx_copy(BW - 1 - a, a).wait_recv()
                put_mx(rmx[a], a)
        ks = slice(b * bs, (b1 + 1) * bs)
        lo_a, hi_a = max(0, b - MID), min(BW - 1, b1 + MID)
        rs = slice(lo_a * bs, (hi_a + 1) * bs)
        y = dot(whi[rs, ks], x2m[ks, :])
        y = y[:, 0:bs] + y[:, bs:2 * bs] + dot(wlo[rs, ks], x2m[ks, 0:bs])
        for a in range(lo_a, hi_a + 1):
            v = y[(a - lo_a) * bs:(a - lo_a + 1) * bs, :]
            oc[1, a] = oc[1, a] + v if a in touched else v
            touched.add(a)
    for a in LEAVE:
        oc[1, a] = oc[1, a] * msk[a:a + 1, :]
        send_out(1, a)

    def finish(which, ref):
        def step(i, _):
            t = own_slot(i)
            ref[i, t] = oc[which, i - c + MID]

            @pl.when(i == c)
            def _():
                ref[i, 0] = jnp.zeros((bs, bs), F32)

            @pl.when(i != c)
            def _():
                pltpu.make_async_remote_copy(
                    src_ref=oc.at[which, 0], dst_ref=ro.at[which, i],
                    send_sem=oss.at[which, 0], recv_sem=ors.at[which, i],
                    device_id=up, device_id_type=MESH,
                ).wait_recv()
                ref[i, 1 - t] = ro[which, i]
            return 0

        lax.fori_loop(0, 8, step, 0)

    finish(0, new_ref)
    finish(1, en_ref)

    for cp in sends:
        cp.wait_send()

    def sent_h(i, _):
        @pl.when(i != c)
        def _():
            h_copy(i).wait_send()
        return 0

    lax.fori_loop(0, 8, sent_h, 0)

    def sent_relay(n, _):
        k = n // 8
        slot = n % 8
        _, _, is_up, is_down = relayed(k, slot, low)

        @pl.when(is_up | is_down)
        def _():
            relay_copy(k, slot, is_up).wait_send()
        return 0

    lax.fori_loop(0, 64, sent_relay, 0)
    for a in range(BW):
        if a != MID:
            mx_copy(a, BW - 1 - a).wait_send()

            @pl.when(leaves(a))
            def _():
                for which in (0, 1):
                    out_copy(which, a).wait_send()

    def cross_sent(slot, _):
        @pl.when(reach(c, slot, 1 - low) > 0)
        def _():
            cross_copy(slot).wait_send()
        return 0

    lax.fori_loop(0, 8, cross_sent, 0)
    for slot in range(8):
        for delta in range(8):
            spread_sent(slot, delta)


def body(density, hamiltonian, neighbours):
    bs = density.shape[-1]
    block = (bs, bs)
    wide = (BW * bs, BW * bs)
    tall = (BW * bs, 2 * bs)
    vm = pl.BlockSpec(memory_space=pltpu.VMEM)
    dma = pltpu.SemaphoreType.DMA
    out = jax.ShapeDtypeStruct(density.shape, F32)
    return pl.pallas_call(
        kernel,
        out_shape=(out, out),
        in_specs=[pl.BlockSpec(memory_space=pltpu.HBM)] * 3,
        out_specs=(vm, vm),
        scratch_shapes=[
            pltpu.VMEM(density.shape, F32),
            pltpu.VMEM(hamiltonian.shape, F32),
            pltpu.VMEM(neighbours.shape, jnp.int32),
            dma((3,)),
            pltpu.VMEM((8, 8) + block, F32),
            pltpu.VMEM((8, 8) + block, F32),
            pltpu.VMEM((8, 8) + block, F32),
            pltpu.VMEM((8,) + block, F32),
            pltpu.VMEM(wide, BF16),
            pltpu.VMEM(wide, BF16),
            pltpu.VMEM(tall, BF16),
            pltpu.VMEM(tall, BF16),
            pltpu.VMEM(tall, BF16),
            pltpu.VMEM(tall, BF16),
            pltpu.VMEM((BW,) + block, F32),
            pltpu.VMEM((BW,) + block, F32),
            pltpu.VMEM((BW,) + block, F32),
            pltpu.VMEM((2, BW) + block, F32),
            pltpu.VMEM((2, 8) + block, F32),
            pltpu.VMEM((24, bs), F32),
            dma((8, 7)), dma((8, 8)),
            dma((8, 8)), dma((8, 8)),
            dma((8, 8, 3)), dma((8, 8)), dma((8,)),
            dma((8,)), dma((8,)),
            dma((BW,)), dma((BW,)),
            dma((2, BW)), dma((2, 8)),
        ],
        compiler_params=pltpu.CompilerParams(
            collective_id=0, has_side_effects=True, vmem_limit_bytes=52 * 2**20
        ),
        cost_estimate=pl.CostEstimate(flops=9 * 10**9, bytes_accessed=4 * 2**20, transcendentals=0),
        name="purify",
    )(density, hamiltonian, neighbours)


def solution(mesh):
    placed = (P("row", "col", None, None), P("row", "col", None, None), P("row", None))
    return jax.shard_map(
        body,
        mesh=mesh,
        in_specs=placed,
        out_specs=(P("row", "col", None, None), P("row", "col", None, None)),
        check_vma=False,
    )
```

```python
import functools
import jax
import jax.numpy as jnp
from jax import lax
from jax.experimental import pallas as pl
from jax.experimental.pallas import tpu as pltpu
from jax.sharding import PartitionSpec as P

MESH = pl.DeviceIdType.MESH
F32 = jnp.float32
BF16 = jnp.bfloat16
R8 = 8
N_ROW = 16
NB = 128
BW = 15
MID = 7
GATHER = tuple(((1, 2, 4), (4, 1, 2), (2, 4, 1))[n % 3] for n in range(8))
SPREAD = ((4, 2, 1), (2, 4, 1), (2, 4, 1), (4, 2, 1), (1, 2, 4), (4, 2, 1), (1, 2, 4), (1, 2, 4))
PAIRS = (6, 8, 4, 10, 2, 12, 0, 14)
LEAVE = (0, 14, 1, 13, 2, 12, 3, 11, 4, 10, 5, 9, 6, 8, 7)


def class_of(c, delta):
    if delta & 1:
        c = c + 1 - 2 * (c % 2)
    if delta & 2:
        c = c + 2 * (1 - 2 * ((c // 2) % 2))
    if delta & 4:
        c = c % 2 + 6 - 2 * (c // 2)
    return c


def slot_row(k, slot):
    if isinstance(slot, int):
        t = k + (slot - 4 if slot > 4 else slot)
    else:
        t = k + jnp.where(slot > 4, slot - 4, slot)
    wrapped = t >= 8
    i = jnp.where(wrapped, t - 8, t)
    if isinstance(slot, int):
        if slot < 4:
            return i, 0
        return i, jnp.where(wrapped, -1, 0 if slot == 4 else 1)
    return i, jnp.where(wrapped & (slot >= 4), -1, jnp.where(slot > 4, 1, 0))


def limits(k, slot):
    i, off = slot_row(k, slot)
    under, over = jnp.minimum(k, i), jnp.maximum(k, i)
    if not isinstance(off, int):
        under = jnp.where(off == 0, under, jnp.where(off > 0, i, 0))
        over = jnp.where(off == 0, over, jnp.where(off < 0, i, 7))
    return i, off, under, over


def dims_after(o, delta):
    last = max([n for n in range(3) if delta & o[n]], default=-1)
    return o[last + 1:]


def subtree(o, delta):
    found = [delta]
    for d in dims_after(o, delta):
        found += [x | d for x in found]
    return found


def split(x):
    hi = x.astype(BF16)
    lo = (x - hi.astype(F32)).astype(BF16)
    return hi, lo


def kernel(
    d_hbm, h_hbm, nb_hbm, new_ref, en_ref,
    d_ref, h_ref, nb_ref, isem,
    gat, rel, ext, hal, whi, wlo, xp, xh, x2s, x2m, sq, mx, rmx, oc, ro, msk,
    gss, grs, rss, rrs, ess, ers, zss, hss, hrs, mss, mrs, oss, ors,
):
    bs = d_ref.shape[-1]
    fetch = [
        pltpu.make_async_copy(src, dst, isem.at[n])
        for n, (src, dst) in enumerate(((nb_hbm, nb_ref), (d_hbm, d_ref), (h_hbm, h_ref)))
    ]
    for cp in fetch:
        cp.start()
    r = lax.axis_index("row")
    c = lax.axis_index("col")
    above = jnp.where(r == N_ROW - 1, 0, r + 1)
    below = jnp.where(r == 0, N_ROW - 1, r - 1)
    up = (above, c)
    down = (below, c)
    cls = [class_of(c, delta) for delta in range(8)]

    def owner(a):
        t = c + 1 + a
        row = jnp.where(t < 8, below, jnp.where(t < 16, r, above))
        return (row, jnp.where(t < 8, t, jnp.where(t < 16, t - 8, t - 16)))

    barrier = pltpu.get_barrier_semaphore()
    for a in range(BW):
        if a != MID:
            pl.semaphore_signal(barrier, inc=1, device_id=owner(a), device_id_type=MESH)
    pl.semaphore_signal(barrier, inc=1, device_id=up, device_id_type=MESH)
    pl.semaphore_signal(barrier, inc=1, device_id=down, device_id_type=MESH)

    def rows(a):
        return pl.ds(pl.multiple_of(a * bs, bs), bs)

    def own_slot(i):
        return jnp.where(i <= c, 1, 0)

    fetch[0].wait()
    col_mine = (8 * r + c - MID + NB + lax.broadcasted_iota(jnp.int32, (16, 16), 0)) % NB
    hit = jnp.where(nb_ref[pl.ds(c, 1), :] == col_mine, 1.0, 0.0).astype(F32)
    msk[0:16, :] = jnp.broadcast_to(jnp.max(hit, axis=1, keepdims=True), (16, bs))
    row_i = lax.broadcasted_iota(jnp.int32, (8, 16), 0)
    col_other = (8 * r + c + NB + jnp.where(row_i > c, 8, -8)) % NB
    hit = jnp.where(nb_ref[...] == col_other, 1.0, 0.0).astype(F32)
    msk[16:24, :] = jnp.broadcast_to(jnp.max(hit, axis=1, keepdims=True), (8, bs))

    def contribute(slot, _):
        i, off = slot_row(c, slot)
        mine = own_slot(i)
        t = jnp.where(off == 0, mine, 1 - mine)
        m = msk[pl.ds(jnp.where(off == 0, i - c + MID, 16 + i), 1), :]
        gat[c, slot] = d_ref[i, t] * m
        return 0

    fetch[1].wait()
    lax.fori_loop(0, 8, contribute, 0)
    pl.semaphore_wait(barrier, 16)

    sends = []
    counts = [0] * 8
    in_x_half = (r // 2) % 4
    low = 1 - lax.rem(r, 2)
    crossing = jnp.where(in_x_half == jnp.where(low == 1, 0, 3), 1, 0)

    def start_forward(slot, delta, dim):
        k = cls[delta]
        cp = pltpu.make_async_remote_copy(
            src_ref=gat.at[k, slot], dst_ref=gat.at[k, slot],
            send_sem=gss.at[slot, counts[slot]], recv_sem=grs.at[slot, delta ^ dim],
            device_id=(r, cls[dim]), device_id_type=MESH,
        )
        counts[slot] += 1
        cp.start()
        sends.append(cp)

    for slot in range(8):
        start_forward(slot, 0, GATHER[slot][0])

    beyond_r = jnp.where(low == 1, below, above)

    def reach(k, slot, is_low):
        i, off, under, over = limits(k, slot)
        found = jnp.where(is_low == 1, under, 7 - over)
        return jnp.where((crossing == 1) | (off != 0), found, 0)

    def cross_copy(slot):
        return pltpu.make_async_remote_copy(
            src_ref=gat.at[c, slot], dst_ref=ext.at[c, slot],
            send_sem=zss.at[slot], recv_sem=ers.at[c, slot],
            device_id=(beyond_r, c), device_id_type=MESH,
        )

    for slot in range(8):
        @pl.when(reach(c, slot, 1 - low) > 0)
        def _():
            cross_copy(slot).start()

    for slot in range(8):
        start_forward(slot, 0, GATHER[slot][1])

    dist = [jnp.where(low == 1, k, 7 - k) for k in cls]
    reached = {}

    def neediest(o, delta, dim):
        nodes = frozenset(delta ^ x for x in subtree(o, delta | dim))
        if nodes not in reached:
            reached[nodes] = functools.reduce(jnp.minimum, [dist[x] for x in sorted(nodes)])
        return reached[nodes]

    mine = dist[0]
    base = jnp.where(low == 1, -8, 8)
    def spread_copy(k, slot, dim, n):
        return pltpu.make_async_remote_copy(
            src_ref=ext.at[k, slot], dst_ref=ext.at[k, slot],
            send_sem=ess.at[k, slot, n], recv_sem=ers.at[k, slot],
            device_id=(r, cls[dim]), device_id_type=MESH,
        )

    onward = {}

    def spread(pick, slots=range(8)):
        for slot in slots:
            o = SPREAD[slot]
            delta = pick(o)
            k = cls[delta]
            here = neediest(o, delta, 0)
            if (o, delta) not in onward:
                onward[o, delta] = [(dim, neediest(o, delta, dim)) for dim in dims_after(o, delta)]
            need = reach(k, slot, low)

            @pl.when(here < need)
            def _():
                spread_copy(k, slot, 1, 0).wait_recv()
                for n, (dim, v) in enumerate(onward[o, delta]):
                    @pl.when(v < need)
                    def _():
                        spread_copy(k, slot, dim, n).start()

    def spread_sent(slot, delta):
        o = SPREAD[slot]
        k = cls[delta]
        need = reach(k, slot, low)
        for n, (dim, v) in enumerate(onward[o, delta]):
            @pl.when((neediest(o, delta, 0) < need) & (v < need))
            def _():
                spread_copy(k, slot, dim, n).wait_send()

    def class_at(orders, pick, slot):
        deltas = [pick(o) for o in orders]
        k = cls[deltas[0]]
        for delta in sorted(set(deltas) - {deltas[0]}):
            hit = functools.reduce(jnp.logical_or, [slot == n for n in range(8) if deltas[n] == delta])
            k = jnp.where(hit, cls[delta], k)
        return k

    def put_spread(pick, slots=range(8)):
        def step(slot, _):
            k = class_at(SPREAD, pick, slot)

            @pl.when(mine < reach(k, slot, low))
            def _():
                i, off = slot_row(k, slot)
                put(ext[k, slot], i - c + MID + base, k + 8 * off - c + MID + base)
            return 0

        lax.fori_loop(slots[0], slots[-1] + 1, step, 0)

    def send_h(i, _):
        @pl.when(i != c)
        def _():
            t = 1 - own_slot(i)
            pltpu.make_async_remote_copy(
                src_ref=h_ref.at[i, t], dst_ref=hal.at[i],
                send_sem=hss.at[i], recv_sem=hrs.at[i],
                device_id=(jnp.where(i > c, above, below), c), device_id_type=MESH,
            ).start()
        return 0

    fetch[2].wait()
    lax.fori_loop(0, 8, send_h, 0)

    def relayed(k, slot, inner_up):
        i, off, under, over = limits(k, slot)
        plain = (off == 0) & (crossing == 0)
        return i, off, (c < under) & (plain | (inner_up == 1)), (c > over) & (plain | (inner_up == 0))

    def relay_copy(k, slot, is_up):
        return pltpu.make_async_remote_copy(
            src_ref=gat.at[k, slot], dst_ref=rel.at[k, slot],
            send_sem=rss.at[k, slot], recv_sem=rrs.at[k, slot],
            device_id=(jnp.where(is_up, above, below), c), device_id_type=MESH,
        )

    def put(x, a, b):
        hi, lo = split(x)
        whi[rows(a), rows(b)] = hi
        wlo[rows(a), rows(b)] = lo
        whi[rows(b), rows(a)] = hi.T
        wlo[rows(b), rows(a)] = lo.T

    def relay(pick):
        for slot in range(8):
            k = cls[pick(GATHER[slot])]
            _, _, is_up, is_down = relayed(k, slot, low)

            @pl.when(is_up | is_down)
            def _():
                relay_copy(k, slot, is_up).start()

    def put_own(pick):
        def step(slot, _):
            k = class_at(GATHER, pick, slot)
            i, off = slot_row(k, slot)
            b = k + 8 * off - c + MID

            @pl.when((b >= 0) & (b < BW))
            def _():
                put(gat[k, slot], i - c + MID, b)
            return 0

        lax.fori_loop(0, 8, step, 0)

    def put_relayed(pick, inner=True, outer=True):
        def step(slot, _):
            k = class_at(GATHER, pick, slot)
            i, off, from_below, from_above = relayed(k, slot, 1 - low)
            if not outer:
                from_below, from_above = from_below & (low == 0), from_above & (low == 1)
            if not inner:
                from_below, from_above = from_below & (low == 1), from_above & (low == 0)

            @pl.when(from_below | from_above)
            def _():
                relay_copy(k, slot, from_below).wait_recv()
                shift = jnp.where(from_below, -8, 8) - c + MID
                put(rel[k, slot], i + shift, k + 8 * off + shift)
            return 0

        lax.fori_loop(0, 8, step, 0)

    w0 = lambda o: 0
    w1 = lambda o: o[0]
    w2 = lambda o: o[1]
    w3 = lambda o: o[2]
    w12 = lambda o: o[0] | o[1]
    w13 = lambda o: o[0] | o[2]
    w23 = lambda o: o[1] | o[2]
    w123 = lambda o: 7
    relay(w0)

    zero = jnp.zeros((bs, bs), BF16)
    for b in range(0, BW, 2):
        b1 = min(b + 1, BW - 1)
        for a in range(max(0, b - MID), min(BW - 1, b1 + MID) + 1):
            for q in (b, b1):
                if abs(a - q) > MID:
                    whi[a * bs:(a + 1) * bs, q * bs:(q + 1) * bs] = zero
                    wlo[a * bs:(a + 1) * bs, q * bs:(q + 1) * bs] = zero
    put_own(w0)

    def arrive(slot, delta):
        k = cls[delta]
        pltpu.make_async_remote_copy(
            src_ref=gat.at[k, slot], dst_ref=gat.at[k, slot],
            send_sem=gss.at[slot, 0], recv_sem=grs.at[slot, delta],
            device_id=(r, cls[1]), device_id_type=MESH,
        ).wait_recv()

    def wave(pick, dims):
        for slot in range(8):
            o = GATHER[slot]
            arrive(slot, pick(o))
            for n in dims:
                start_forward(slot, pick(o), o[n])

    wave(w1, (1,))
    for slot in range(8):
        start_forward(slot, 0, GATHER[slot][2])
        start_forward(slot, GATHER[slot][0], GATHER[slot][2])
    relay(w1)
    spread(w0)
    put_relayed(w0)
    put_own(w1)
    wave(w2, (2,))
    relay(w2)
    spread(w1)
    put_relayed(w1)
    wave(w12, (2,))
    relay(w12)
    wave(w3, ())
    relay(w3)
    spread(w2)
    put_own(w2)
    put_spread(w0)
    spread(w12)
    put_spread(w1)
    put_own(w12)
    put_own(w3)
    put_relayed(w2)
    diag = range(0, 4)
    rest = range(4, 8)
    put_relayed(w12, outer=False)
    put_spread(w2)
    wave(w13, ())
    relay(w13)
    put_own(w13)
    put_spread(w12)
    put_relayed(w3, outer=False)
    wave(w23, ())
    relay(w23)
    put_own(w23)
    put_relayed(w13, outer=False)
    wave(w123, ())
    relay(w123)
    put_own(w123)
    put_relayed(w23, outer=False)
    for w in (w3, w13, w23, w123):
        spread(w, rest)
        put_spread(w, rest)
    put_relayed(w123, outer=False)

    def outer_diagonal():
        for w in (w12, w3, w13):
            put_relayed(w, inner=False)
        for w in (w3, w13, w23, w123):
            spread(w, diag)
            put_spread(w, diag)
        for w in (w23, w123):
            put_relayed(w, inner=False)

    def put_h(x, a):
        hi, lo = split(x * msk[pl.ds(a, 1), :])
        xh[rows(a), 0:bs] = hi
        xh[rows(a), bs:2 * bs] = lo

    def h_copy(i):
        return pltpu.make_async_remote_copy(
            src_ref=h_ref.at[i, 0], dst_ref=hal.at[i],
            send_sem=hss.at[i], recv_sem=hrs.at[i],
            device_id=up, device_id_type=MESH,
        )

    def take_h(i, _):
        put_h(h_ref[i, own_slot(i)], i - c + MID)

        @pl.when(i != c)
        def _():
            h_copy(i).wait_recv()
            put_h(hal[i], i - c + jnp.where(i > c, -1, 15))
        return 0

    lax.fori_loop(0, 8, take_h, 0)


    dot = functools.partial(jnp.dot, preferred_element_type=F32)

    def band(a):
        lo_b, hi_b = max(0, a - MID), min(BW - 1, a + MID)
        return slice(a * bs, (a + 1) * bs), slice(lo_b * bs, (hi_b + 1) * bs)

    def mx_copy(a, back):
        return pltpu.make_async_remote_copy(
            src_ref=mx.at[a], dst_ref=rmx.at[back],
            send_sem=mss.at[a], recv_sem=mrs.at[back],
            device_id=owner(a), device_id_type=MESH,
        )

    def half(a, v):
        rs, ks = band(a)
        y = dot(whi[rs, ks], v[ks, :])
        return y[:, 0:bs] + y[:, bs:2 * bs] + dot(wlo[rs, ks], v[ks, 0:bs])

    def first_product(some):
        for a in some:
            mx[a] = half(a, xh) * msk[a:a + 1, :]
            if a != MID:
                mx_copy(a, BW - 1 - a).start()

    @pl.when(low == 1)
    def _():
        first_product(range(BW - 1, MID - 1, -1))

    @pl.when(low == 0)
    def _():
        first_product(range(0, MID + 1))

    outer_diagonal()

    @pl.when(low == 1)
    def _():
        first_product(range(MID - 1, -1, -1))

    @pl.when(low == 0)
    def _():
        first_product(range(MID + 1, BW))

    xp[:, 0:bs] = whi[:, MID * bs:(MID + 1) * bs]
    xp[:, bs:2 * bs] = wlo[:, MID * bs:(MID + 1) * bs]
    for a in LEAVE:
        x = half(a, xp) * msk[a:a + 1, :]
        sq[a] = x
        hi, lo = split(x)
        x2s[a * bs:(a + 1) * bs, 0:bs] = hi
        x2s[a * bs:(a + 1) * bs, bs:2 * bs] = lo

    def out_copy(which, a):
        row, i = owner(a)
        return pltpu.make_async_remote_copy(
            src_ref=oc.at[which, a], dst_ref=ro.at[which, i],
            send_sem=oss.at[which, a], recv_sem=ors.at[which, i],
            device_id=(row, c), device_id_type=MESH,
        )

    def leaves(a):
        return (c + 1 + a < 8) | (c + 1 + a >= 16)

    def send_out(which, a):
        if a != MID:
            @pl.when(leaves(a))
            def _():
                out_copy(which, a).start()

    for a in LEAVE:
        y = half(a, x2s)
        oc[0, a] = 3.0 * sq[a] - 2.0 * (y * msk[a:a + 1, :])
        send_out(0, a)

    def put_mx(x, a):
        hi, lo = split(x)
        x2m[rows(a), 0:bs] = hi.T
        x2m[rows(a), bs:2 * bs] = lo.T

    put_mx(mx[MID], MID)
    touched = set()
    for b in PAIRS:
        b1 = min(b + 1, BW - 1)
        for a in range(b, b1 + 1):
            if a != MID:
                mx_copy(BW - 1 - a, a).wait_recv()
                put_mx(rmx[a], a)
        ks = slice(b * bs, (b1 + 1) * bs)
        lo_a, hi_a = max(0, b - MID), min(BW - 1, b1 + MID)
        rs = slice(lo_a * bs, (hi_a + 1) * bs)
        y = dot(whi[rs, ks], x2m[ks, :])
        y = y[:, 0:bs] + y[:, bs:2 * bs] + dot(wlo[rs, ks], x2m[ks, 0:bs])
        for a in range(lo_a, hi_a + 1):
            v = y[(a - lo_a) * bs:(a - lo_a + 1) * bs, :]
            oc[1, a] = oc[1, a] + v if a in touched else v
            touched.add(a)
    for a in LEAVE:
        oc[1, a] = oc[1, a] * msk[a:a + 1, :]
        send_out(1, a)

    def finish(which, ref):
        def step(i, _):
            t = own_slot(i)
            ref[i, t] = oc[which, i - c + MID]

            @pl.when(i == c)
            def _():
                ref[i, 0] = jnp.zeros((bs, bs), F32)

            @pl.when(i != c)
            def _():
                pltpu.make_async_remote_copy(
                    src_ref=oc.at[which, 0], dst_ref=ro.at[which, i],
                    send_sem=oss.at[which, 0], recv_sem=ors.at[which, i],
                    device_id=up, device_id_type=MESH,
                ).wait_recv()
                ref[i, 1 - t] = ro[which, i]
            return 0

        lax.fori_loop(0, 8, step, 0)

    finish(0, new_ref)
    finish(1, en_ref)

    for cp in sends:
        cp.wait_send()

    def sent_h(i, _):
        @pl.when(i != c)
        def _():
            h_copy(i).wait_send()
        return 0

    lax.fori_loop(0, 8, sent_h, 0)

    def sent_relay(n, _):
        k = n // 8
        slot = n % 8
        _, _, is_up, is_down = relayed(k, slot, low)

        @pl.when(is_up | is_down)
        def _():
            relay_copy(k, slot, is_up).wait_send()
        return 0

    lax.fori_loop(0, 64, sent_relay, 0)
    for a in range(BW):
        if a != MID:
            mx_copy(a, BW - 1 - a).wait_send()

            @pl.when(leaves(a))
            def _():
                for which in (0, 1):
                    out_copy(which, a).wait_send()

    def cross_sent(slot, _):
        @pl.when(reach(c, slot, 1 - low) > 0)
        def _():
            cross_copy(slot).wait_send()
        return 0

    lax.fori_loop(0, 8, cross_sent, 0)
    for slot in range(8):
        for delta in range(8):
            spread_sent(slot, delta)


def body(density, hamiltonian, neighbours):
    bs = density.shape[-1]
    block = (bs, bs)
    wide = (BW * bs, BW * bs)
    tall = (BW * bs, 2 * bs)
    vm = pl.BlockSpec(memory_space=pltpu.VMEM)
    dma = pltpu.SemaphoreType.DMA
    out = jax.ShapeDtypeStruct(density.shape, F32)
    return pl.pallas_call(
        kernel,
        out_shape=(out, out),
        in_specs=[pl.BlockSpec(memory_space=pltpu.HBM)] * 3,
        out_specs=(vm, vm),
        scratch_shapes=[
            pltpu.VMEM(density.shape, F32),
            pltpu.VMEM(hamiltonian.shape, F32),
            pltpu.VMEM(neighbours.shape, jnp.int32),
            dma((3,)),
            pltpu.VMEM((8, 8) + block, F32),
            pltpu.VMEM((8, 8) + block, F32),
            pltpu.VMEM((8, 8) + block, F32),
            pltpu.VMEM((8,) + block, F32),
            pltpu.VMEM(wide, BF16),
            pltpu.VMEM(wide, BF16),
            pltpu.VMEM(tall, BF16),
            pltpu.VMEM(tall, BF16),
            pltpu.VMEM(tall, BF16),
            pltpu.VMEM(tall, BF16),
            pltpu.VMEM((BW,) + block, F32),
            pltpu.VMEM((BW,) + block, F32),
            pltpu.VMEM((BW,) + block, F32),
            pltpu.VMEM((2, BW) + block, F32),
            pltpu.VMEM((2, 8) + block, F32),
            pltpu.VMEM((24, bs), F32),
            dma((8, 7)), dma((8, 8)),
            dma((8, 8)), dma((8, 8)),
            dma((8, 8, 3)), dma((8, 8)), dma((8,)),
            dma((8,)), dma((8,)),
            dma((BW,)), dma((BW,)),
            dma((2, BW)), dma((2, 8)),
        ],
        compiler_params=pltpu.CompilerParams(
            collective_id=0, has_side_effects=True, vmem_limit_bytes=52 * 2**20
        ),
        cost_estimate=pl.CostEstimate(flops=9 * 10**9, bytes_accessed=4 * 2**20, transcendentals=0),
        name="purify",
    )(density, hamiltonian, neighbours)


def solution(mesh):
    placed = (P("row", "col", None, None), P("row", "col", None, None), P("row", None))
    return jax.shard_map(
        body,
        mesh=mesh,
        in_specs=placed,
        out_specs=(P("row", "col", None, None), P("row", "col", None, None)),
        check_vma=False,
    )
```
